32 devices in a mesh: src: 2 (over y), width: 16 (over z, x, core).
Axes of the slice: x: 2, y: 2, z: 4, core: 2. Of those that a mesh axis runs over, the one named last changes fastest.
Arguments:
- resid: bfloat16 [2, 512, 8192], P('src', None, 'width'), may hold values from -6 to 6
- enc_w: bfloat16 [2, 8192, 6144], P('src', 'width'), may hold values from -0.0625 to 0.0625
- enc_b: float32 [2, 6144], P('src'), may hold values from -3 to 3
- dec_w: bfloat16 [2, 6144, 8192], P('src', None, 'width'), may hold values from -0.078125 to 0.078125
- target: bfloat16 [512, 8192], P(None, 'width'), may hold values from -36 to 36
- norm_gain: float32 [8192], P('width'), may hold values from 0.5 to 1.5
- wq: bfloat16 [8192, 4096], P(None, 'width'), may hold values from -0.0625 to 0.0625
- wk: bfloat16 [8192, 512], P('width'), may hold values from -0.0625 to 0.0625
- wv: bfloat16 [8192, 512], P('width'), may hold values from -0.0625 to 0.0625
- prompt_ids: int32 [512], replicated, may hold values from 0 to 3, never falling along the last dimension, each value on 1 to 256 neighbouring positions
Outputs:
- mlp_out: bfloat16 [512, 8192], P('src', 'width')
- context: bfloat16 [512, 4096], P('src', 'width')
The draws below stay inside these ranges and needn't reach their ends.
Inputs may be any that keep to these rules, and one draw needn't show every extreme that they name: `prompt_ids`: rows of one prompt are contiguous and numbered in increasing order; the longest prompt has 256 rows.
All inputs are finite; a program needn't handle non-finite values.
Results may differ from the reference program's by a relative error of at most 0.008.
Values may be sent and summed in bfloat16 or wider, within the bound.
A program may use at most 128 MiB of HBM per device.

```python
import math
import jax
import jax.numpy as jnp
import numpy as np
from jax import lax

D = 8192
HD = 128
GROUP = 8
F = 6144
ROWS = 512
LAYERS = 2
HEADS = 32
KV = 4


def draw_target(key, part):
    first, second = jax.random.split(key, 2)
    columns = 1.0 + 2.0 * jnp.arange(D, dtype=jnp.float32) / D
    row_scale = jnp.exp(jax.random.uniform(second, (ROWS, 1), jnp.float32, math.log(0.3), math.log(3.0)))
    base = jnp.clip(jax.random.normal(first, (ROWS, D), jnp.float32), -4.0, 4.0)
    return (base * columns[None, :] * row_scale).astype(jnp.bfloat16)


def steps_of(rng, dims, cuts, least, largest):
    factor_of, own = 1.0, jax.random.fold_in(rng, 6)
    for axis_at, parts in cuts:
        steps = jnp.exp(jax.random.uniform(jax.random.fold_in(own, axis_at), (parts,), jnp.float32, least / len(cuts), largest / len(cuts)))
        factor_of = factor_of * jnp.repeat(steps, dims[axis_at] // parts).reshape([-1 if axis == axis_at else 1 for axis in range(len(dims))])
    return factor_of


def profile(number_of, total, limit, lean):
    portions = [(1 << 20) // math.isqrt(rank ** lean) + 1 for rank in range(2, number_of + 1)]
    spare, given = total - limit - (number_of - 1), [1] * (number_of - 1)
    while spare > 0:
        movable = [i for i in range(number_of - 1) if given[i] < limit]
        pool, remaining = sum([portions[i] for i in movable]), spare
        for i in movable:
            addition = min(limit - given[i], max(1, remaining * portions[i] // pool), spare)
            given[i] = given[i] + addition
            spare = spare - addition
    return np.array([limit] + given)


def ragged(key, number_of, total, reach, slope):
    if number_of == 2:
        one = jax.random.randint(key, (), max(1, total - reach), min(reach, total - 1) + 1)
        return jnp.stack([one, total - one])
    sizes = jnp.asarray(profile(number_of, total, reach, slope), jnp.int32)
    twos = (number_of - 1) // 2
    source_of, taker = sizes[1:1 + 2 * twos:2], sizes[2:2 + 2 * twos:2]
    margin = jnp.minimum(source_of - 1, reach - taker)
    moved = jax.random.randint(jax.random.fold_in(key, 1), (twos,), 0, 1 << 20) % (margin + 1)
    sizes = sizes.at[1:1 + 2 * twos:2].set(source_of - moved).at[2:2 + 2 * twos:2].set(taker + moved)
    return sizes[jax.random.permutation(jax.random.fold_in(key, 2), number_of)]


def gaussian(rng, extent, deviation, limit, shards=(), held_as=jnp.bfloat16):
    loudness = steps_of(rng, extent, shards, -0.22, 0.18) if shards else 1.0
    drawn = jax.random.normal(rng, extent, jnp.float32) * deviation * loudness
    return jnp.minimum(jnp.maximum(drawn, -limit), limit).astype(held_as)


def setup_inputs(seed: int = 0) -> dict:
    key_of = jax.random.split(jax.random.key(seed), 11)
    resid = gaussian(key_of[0], (LAYERS, ROWS, D), 1.0, 6.0, ((0, 2), (2, 16)))
    enc_w = gaussian(key_of[1], (LAYERS, D, F), D ** -0.5, 0.0625, ((0, 2), (1, 16)))
    enc_b = gaussian(key_of[2], (LAYERS, F), 0.5, 3.0, ((0, 2),), jnp.float32)
    dec_w = gaussian(key_of[3], (LAYERS, F, D), F ** -0.5, 0.078125, ((0, 2), (2, 16)))
    target = draw_target(jax.random.fold_in(key_of[10], 71), 0)
    norm_gain = jnp.clip(0.5 + 1.0 * jax.random.uniform(key_of[5], (D,), jnp.float32) ** steps_of(key_of[5], (D,), ((0, 16),), -0.2, 0.2), 0.5, 1.5)
    wq = gaussian(key_of[6], (D, HEADS * HD), D ** -0.5, 0.0625, ((1, 16),))
    wk = gaussian(key_of[7], (D, KV * HD), D ** -0.5, 0.0625, ((0, 16),))
    wv = gaussian(key_of[8], (D, KV * HD), D ** -0.5, 0.0625, ((0, 16),))
    prompt_ids = jnp.searchsorted(jnp.cumsum(ragged(key_of[9], max(ROWS // 128, 4), ROWS, ROWS // 2, 2)), jnp.arange(ROWS), side="right").astype(jnp.int32)
    return {"resid": resid, "enc_w": enc_w, "enc_b": enc_b, "dec_w": dec_w, "target": target, "norm_gain": norm_gain, "wq": wq, "wk": wk, "wv": wv, "prompt_ids": prompt_ids}


def reference(resid, enc_w, enc_b, dec_w, target, norm_gain, wq, wk, wv, prompt_ids):

    def layer_step(total, inputs):
        rows, w_enc, bias, w_dec = inputs
        pre = jnp.dot(rows, w_enc, preferred_element_type=jnp.float32)
        feats = jnp.maximum(pre + bias[None, :], 0.0).astype(jnp.bfloat16)
        return (total + jnp.dot(feats, w_dec, preferred_element_type=jnp.float32), None)
    mlp, _ = lax.scan(layer_step, jnp.zeros((ROWS, D), jnp.float32), (resid, enc_w, enc_b, dec_w))
    mlp_out = mlp.astype(jnp.bfloat16)
    stream = target.astype(jnp.float32) + mlp
    power = lax.optimization_barrier(jnp.mean(stream * stream, axis=1, keepdims=True))
    normed = (stream * lax.rsqrt(power + 1e-05) * norm_gain[None, :]).astype(jnp.bfloat16)
    query = jnp.dot(normed, wq, preferred_element_type=jnp.float32).astype(jnp.bfloat16)
    keys = jnp.dot(normed, wk, preferred_element_type=jnp.float32).astype(jnp.bfloat16)
    values = jnp.dot(normed, wv, preferred_element_type=jnp.float32).astype(jnp.bfloat16)
    index = jnp.arange(ROWS, dtype=jnp.int32)
    allowed = (prompt_ids[:, None] == prompt_ids[None, :]) & (index[None, :] <= index[:, None])
    query4 = query.reshape(ROWS, KV, GROUP, HD).astype(jnp.float32)
    keys3 = keys.reshape(ROWS, KV, HD).astype(jnp.float32)
    values3 = values.reshape(ROWS, KV, HD).astype(jnp.float32)
    scores = jnp.einsum('qkgd,skd->kgqs', query4, keys3) / math.sqrt(HD)
    scores = jnp.where(allowed[None, None], scores, -1e+30)
    peak = lax.optimization_barrier(jnp.max(scores, axis=-1, keepdims=True))
    weights = jnp.exp(scores - peak)
    probs = (weights / lax.optimization_barrier(jnp.sum(weights, axis=-1, keepdims=True))).astype(jnp.bfloat16)
    context = jnp.einsum('kgqs,skd->qkgd', probs.astype(jnp.float32), values3)
    return (mlp_out, context.reshape(ROWS, HEADS * HD).astype(jnp.bfloat16))
```

```python
import functools
import math

import jax
import jax.numpy as jnp
from jax import lax
from jax.experimental import pallas as pl
from jax.experimental.pallas import tpu as pltpu
from jax.sharding import PartitionSpec as P

HD = 128
GROUP = 8
NC = 2
NZ = 4
T = 4
BF = jnp.bfloat16
F32 = jnp.float32


def dot(a, b):
    return jnp.dot(a, b, preferred_element_type=F32)


def kernel(
    n, n_src,
    resid, enc_w, enc_b, dec_w, target, gain, wq, wk, wv, ids_row, ids_col,
    mlp_out, context,
    rs_v, e_v, d_v, t_v, q_v, k_v, v_v,
    part, c_buf, x_buf, z_buf, feats, acc, y_send, y_buf,
    full, pw, r_col, kvp, kvr, kv, qacc,
    load_sem, c_sem, x_sem, z_sem, gz_sem, gx_sem, gc_sem, y_sem, f_sem, p_sem, kr_sem, kg_sem,
):
    nx = n // (NC * NZ)
    rows = resid.shape[1]
    share = resid.shape[2]
    fc = enc_w.shape[2] // T
    R = rows // n_src
    H, X, Z = rows // NC, rows // (NC * nx), rows // n
    w = lax.axis_index("width")
    s = lax.axis_index("src")
    c = lax.rem(w, NC)
    x = lax.rem(w // NC, nx)
    z = w // (NC * nx)
    members = 4
    g, m = w // members, lax.rem(w, members)
    n_kv = n // members
    RQ = R // members

    def wid(zz, xx, cc):
        return (zz * nx + xx) * NC + cc

    def plus(v, k, size):
        return lax.rem(v + k, size)

    def minus(v, k, size):
        return lax.rem(v + size - k, size)

    def ds(start, size):
        return pl.ds(pl.multiple_of(start, size), size)

    loads = []

    def load(i, src, dst):
        cp = pltpu.make_async_copy(src, dst, load_sem.at[i])
        cp.start()
        loads.append(cp)
        return cp

    ld_resid = load(0, resid.at[0], rs_v)
    ld_e = [load(1 + t, enc_w.at[0, :, pl.ds(t * fc, fc)], e_v.at[t]) for t in range(T)]
    ld_d = load(T + 1, dec_w.at[0], d_v)
    ld_t = load(T + 2, target.at[ds(s * R, R)], t_v)
    ld_k = load(T + 3, wk, k_v)
    ld_v = load(T + 4, wv, v_v)
    ld_q = load(T + 5, wq, q_v)

    barrier = pltpu.get_barrier_semaphore()
    for k in range(1, n):
        pl.semaphore_signal(barrier, inc=1, device_id={"src": s, "width": plus(w, k, n)})
    for ks in range(1, n_src):
        for mm in range(members):
            pl.semaphore_signal(
                barrier, inc=1,
                device_id={"src": plus(s, ks, n_src), "width": g * members + mm},
            )

    sends = []

    def rdma(src, dst, sems, i, dev):
        return pltpu.make_async_remote_copy(
            src_ref=src, dst_ref=dst, send_sem=sems.at[(0,) + i], recv_sem=sems.at[(1,) + i],
            device_id=dev, device_id_type=pl.DeviceIdType.MESH,
        )

    def send(src, dst, sems, i, ww=None, ss=None):
        cp = rdma(src, dst, sems, i, {"src": s if ss is None else ss, "width": w if ww is None else ww})
        cp.start()
        sends.append(cp)

    def arrive(dst, sems, i):
        rdma(dst, dst, sems, i, {"src": s, "width": plus(w, 1, n)}).wait_recv()

    sibling = wid(z, x, 1 - c)
    c0 = c * H
    x0 = c0 + x * X
    z0 = x0 + z * Z

    def encode(t):
        ld_e[t].wait()
        step = 512 if fc % 512 == 0 else fc

        @pl.loop(0, fc // step)
        def _(j):
            cols = ds(j * step, step)
            part[t, :, cols] = dot(rs_v[...], e_v[t, :, cols]).astype(BF)

    def rs_c(t):
        send(part.at[t, ds((1 - c) * H, H)], c_buf.at[t], c_sem, (t,), sibling)

    def rs_x(t):
        arrive(c_buf.at[t], c_sem, (t,))

        def add(xx):
            @pl.loop(0, X // Z)
            def _(j):
                a = ds(c0 + xx * X + j * Z, Z)
                b = ds(xx * X + j * Z, Z)
                part[t, a] = (part[t, a].astype(F32) + c_buf[t, b].astype(F32)).astype(BF)

        for k in range(1, nx):
            xx = plus(x, k, nx)
            add(xx)
            send(part.at[t, ds(c0 + xx * X, X)], x_buf.at[t, k - 1], x_sem, (t, k - 1), wid(z, xx, c))
        add(x)

    def rs_z(t):
        for k in range(1, nx):
            arrive(x_buf.at[t, k - 1], x_sem, (t, k - 1))

        def add(zz):
            a = ds(x0 + zz * Z, Z)
            b = ds(zz * Z, Z)
            total = part[t, a].astype(F32)
            for k in range(1, nx):
                total += x_buf[t, k - 1, b].astype(F32)
            part[t, a] = total.astype(BF)

        for k in (2, 1, 3):
            zz = plus(z, k, NZ)
            add(zz)
            send(part.at[t, ds(x0 + zz * Z, Z)], z_buf.at[t, k - 1], z_sem, (t, k - 1), wid(zz, x, c))
        add(z)

    def ag_z(t):
        for k in range(1, NZ):
            arrive(z_buf.at[t, k - 1], z_sem, (t, k - 1))
        own = ds(z0, Z)
        total = part[t, own].astype(F32) + enc_b[:, pl.ds(t * fc, fc)]
        for k in range(1, NZ):
            total += z_buf[t, k - 1].astype(F32)
        feats[t, own] = jnp.maximum(total, 0.0).astype(BF)
        for k in (2, 1, 3):
            send(feats.at[t, own], feats.at[t, own], gz_sem, (t, k - 1), wid(plus(z, k, NZ), x, c))

    def ag_x(t):
        for k in range(1, NZ):
            arrive(feats.at[t, ds(x0 + minus(z, k, NZ) * Z, Z)], gz_sem, (t, k - 1))
        own = ds(x0, X)
        for k in range(1, nx):
            send(feats.at[t, own], feats.at[t, own], gx_sem, (t, k - 1), wid(z, plus(x, k, nx), c))

    def ag_c(t):
        for k in range(1, nx):
            arrive(feats.at[t, ds(c0 + minus(x, k, nx) * X, X)], gx_sem, (t, k - 1))
        own = ds(c0, H)
        send(feats.at[t, own], feats.at[t, own], gc_sem, (t,), sibling)

    def decode_rows(t, start):
        r = ds(start, R)
        p = dot(feats[t, r], d_v[pl.ds(t * fc, fc), :])
        if t == 0:
            acc[r, :] = p
        else:
            acc[r, :] += p

    def decode(t):
        arrive(feats.at[t, ds((1 - c) * H, H)], gc_sem, (t,))
        if t == 0:
            ld_d.wait()
        for k in range(1, n_src):
            ss = plus(s, k, n_src)
            decode_rows(t, ss * R)
            if t == T - 1:
                y_send[k - 1] = acc[ds(ss * R, R), :].astype(BF)
                send(y_send.at[k - 1], y_buf.at[k - 1], y_sem, (k - 1,), None, ss)
        decode_rows(t, s * R)

    ld_resid.wait()
    encode(0)
    pl.semaphore_wait(barrier, n - 1 + (n_src - 1) * members)
    rs_c(0)
    for t in range(1, T):
        encode(t)
        rs_c(t)
    stages = (rs_x, rs_z, ag_z, ag_x, ag_c, decode)
    for tick in range(T + len(stages) - 1):
        for i in reversed(range(len(stages))):
            if 0 <= tick - i < T:
                stages[i](tick - i)

    for k in range(1, n_src):
        arrive(y_buf.at[k - 1], y_sem, (k - 1,))
    mlp = acc[ds(s * R, R), :]
    for k in range(1, n_src):
        mlp += y_buf[k - 1].astype(F32)
    mlp_out[...] = mlp.astype(BF)
    ld_t.wait()
    stream = t_v[...].astype(F32) + mlp

    def slot(cc, xx, zz):
        return (cc * nx + xx) * NZ + zz

    me = slot(c, x, z)
    full[me] = (stream * gain[...]).astype(BF)

    def forward(cc_done, kx, kz, at):
        if kx == 0:
            for k in range(1, nx):
                send(full.at[at], full.at[at], f_sem, (0, k, kz), wid(z, plus(x, k, nx), c))
        send(full.at[at], full.at[at], f_sem, (1, kx, kz), sibling)

    for k in (2, 1, 3):
        send(full.at[me], full.at[me], f_sem, (0, 0, k), wid(plus(z, k, NZ), x, c))
    forward(0, 0, 0, me)

    sq = lax.dot_general(
        jnp.ones((8, share), F32), stream * stream, (((1,), (1,)), ((), ())),
        precision=lax.Precision.HIGHEST, preferred_element_type=F32,
    )
    pw[0] = sq
    for k in range(1, n):
        send(pw.at[0], pw.at[k], p_sem, (k - 1,), plus(w, k, n))

    ld_k.wait()
    ld_v.wait()
    kp = dot(full[me], k_v[...]).astype(BF)
    vp = dot(full[me], v_v[...]).astype(BF)
    for h in range(n_kv):
        kvp[h, :, 0:HD] = kp[:, h * HD:(h + 1) * HD]
        kvp[h, :, HD:2 * HD] = vp[:, h * HD:(h + 1) * HD]
    for k in range(1, n):
        ww = plus(w, k, n)
        send(kvp.at[ww // members, ds(lax.rem(ww, members) * RQ, RQ)], kvr.at[k - 1], kr_sem, (k - 1,), ww)

    def add_query(at, origin):
        qacc[...] += dot(full[at], q_v[ds(origin * share, share), :])

    ld_q.wait()
    qacc[...] = dot(full[me], q_v[ds(w * share, share), :])
    for kz in (1, 2, 3):
        zz = minus(z, kz, NZ)
        at = slot(c, x, zz)
        arrive(full.at[at], f_sem, (0, 0, kz))
        forward(0, 0, kz, at)
        add_query(at, wid(zz, x, c))

    total = pw[0]
    for k in range(1, n):
        arrive(pw.at[k], p_sem, (k - 1,))
    for k in range(1, n):
        total += pw[k]
    r_col[...] = jnp.transpose(lax.rsqrt(total / (share * n) + 1e-05))
    for k in range(1, n):
        arrive(kvr.at[k - 1], kr_sem, (k - 1,))
    mine = kvp[g, ds(m * RQ, RQ)].astype(F32)
    for k in range(1, n):
        mine += kvr[k - 1].astype(F32)
    out_rows = ds(s * R + m * RQ, RQ)
    kv[out_rows, :] = (mine * r_col[ds(m * RQ, RQ), 0:1]).astype(BF)
    for ks in range(n_src):
        for km in range(members):
            if ks or km:
                send(
                    kv.at[out_rows], kv.at[out_rows], kg_sem, (ks, km),
                    g * members + plus(m, km, members), plus(s, ks, n_src),
                )

    for kx in range(1, nx):
        xx = minus(x, kx, nx)
        for kz in range(NZ):
            zz = minus(z, kz, NZ)
            at = slot(c, xx, zz)
            arrive(full.at[at], f_sem, (0, kx, kz))
            forward(0, kx, kz, at)
            add_query(at, wid(zz, xx, c))
    for kx in range(nx):
        xx = minus(x, kx, nx)
        for kz in range(NZ):
            zz = minus(z, kz, NZ)
            at = slot(1 - c, xx, zz)
            arrive(full.at[at], f_sem, (1, kx, kz))
            add_query(at, wid(zz, xx, 1 - c))

    for ks in range(n_src):
        for km in range(members):
            if ks or km:
                at = minus(s, ks, n_src) * R + minus(m, km, members) * RQ
                arrive(kv.at[ds(at, RQ)], kg_sem, (ks, km))

    query = (qacc[...] * r_col[:, 0:1]).astype(BF)
    qi = s * R + lax.broadcasted_iota(jnp.int32, (R, rows), 0)
    ki = lax.broadcasted_iota(jnp.int32, (R, rows), 1)
    allowed = (ids_col[...] == ids_row[...]) & (ki <= qi)
    for h in range(query.shape[1] // HD):
        scores = lax.dot_general(
            query[:, h * HD:(h + 1) * HD], kv[:, 0:HD], (((1,), (1,)), ((), ())),
            preferred_element_type=F32,
        ) * (1.0 / math.sqrt(HD))
        scores = jnp.where(allowed, scores, -1e30)
        peak = jnp.max(scores, axis=-1, keepdims=True)
        weights = jnp.exp(scores - peak)
        probs = (weights / jnp.sum(weights, axis=-1, keepdims=True)).astype(BF)
        context[:, h * HD:(h + 1) * HD] = dot(probs, kv[:, HD:2 * HD]).astype(BF)

    for cp in sends:
        cp.wait_send()


def on_device(resid, enc_w, enc_b, dec_w, target, norm_gain, wq, wk, wv, prompt_ids):
    n = lax.axis_size("width")
    n_src = lax.axis_size("src")
    rows, share = resid.shape[1:]
    fc = enc_w.shape[2] // T
    R = rows // n_src
    nx = n // (NC * NZ)
    H, X, Z = rows // NC, rows // (NC * nx), rows // n
    members = 4
    n_kv = n // members
    RQ = R // members
    ids_col = lax.dynamic_slice_in_dim(prompt_ids, lax.axis_index("src") * R, R, 0)[:, None]
    any_ = pl.BlockSpec(memory_space=pl.ANY)
    vm = pl.BlockSpec(memory_space=pltpu.VMEM)
    dma = pltpu.SemaphoreType.DMA
    nx1 = max(nx - 1, 1)
    ns1 = max(n_src - 1, 1)
    return pl.pallas_call(
        functools.partial(kernel, n, n_src),
        out_shape=(
            jax.ShapeDtypeStruct((R, share), BF),
            jax.ShapeDtypeStruct((R, wq.shape[1]), BF),
        ),
        in_specs=[any_, any_, vm, any_, any_, vm, any_, any_, any_, vm, vm],
        out_specs=(vm, vm),
        scratch_shapes=[
            pltpu.VMEM((rows, share), BF),
            pltpu.VMEM((T, share, fc), BF),
            pltpu.VMEM((T * fc, share), BF),
            pltpu.VMEM((R, share), BF),
            pltpu.VMEM(wq.shape, BF),
            pltpu.VMEM(wk.shape, BF),
            pltpu.VMEM(wv.shape, BF),
            pltpu.VMEM((T, rows, fc), BF),
            pltpu.VMEM((T, H, fc), BF),
            pltpu.VMEM((T, nx1, X, fc), BF),
            pltpu.VMEM((T, NZ - 1, Z, fc), BF),
            pltpu.VMEM((T, rows, fc), BF),
            pltpu.VMEM((rows, share), F32),
            pltpu.VMEM((ns1, R, share), BF),
            pltpu.VMEM((ns1, R, share), BF),
            pltpu.VMEM((n, R, share), BF),
            pltpu.VMEM((n, 8, R), F32),
            pltpu.VMEM((R, 8), F32),
            pltpu.VMEM((n_kv, R, 2 * HD), BF),
            pltpu.VMEM((n - 1, RQ, 2 * HD), BF),
            pltpu.VMEM((rows, 2 * HD), BF),
            pltpu.VMEM((R, wq.shape[1]), F32),
            dma((T + 6,)),
            dma((2, T)),
            dma((2, T, nx1)),
            dma((2, T, NZ - 1)),
            dma((2, T, NZ - 1)),
            dma((2, T, nx1)),
            dma((2, T)),
            dma((2, ns1)),
            dma((2, 2, nx, NZ)),
            dma((2, n - 1)),
            dma((2, n - 1)),
            dma((2, n_src, members)),
        ],
        compiler_params=pltpu.CompilerParams(
            collective_id=0, has_side_effects=True, vmem_limit_bytes=60 * 1024 * 1024
        ),
    )(resid, enc_w, enc_b, dec_w, target, norm_gain[None, :], wq, wk, wv, prompt_ids[None, :], ids_col)


def solution(mesh):
    in_specs = (
        P("src", None, "width"),
        P("src", "width", None),
        P("src", None),
        P("src", None, "width"),
        P(None, "width"),
        P("width"),
        P(None, "width"),
        P("width", None),
        P("width", None),
        P(),
    )
    out_specs = (P("src", "width"), P("src", "width"))
    return jax.shard_map(
        on_device, mesh=mesh, in_specs=in_specs, out_specs=out_specs, check_vma=False
    )
```

```python
import functools
import math

import jax
import jax.numpy as jnp
from jax import lax
from jax.experimental import pallas as pl
from jax.experimental.pallas import tpu as pltpu
from jax.sharding import PartitionSpec as P

HD = 128
GROUP = 8
NC = 2
NZ = 4
T = 6
BF = jnp.bfloat16
F32 = jnp.float32


def dot(a, b):
    return jnp.dot(a, b, preferred_element_type=F32)


def kernel(
    n, n_src,
    resid, enc_w, enc_b, dec_w, target, gain, wq, wk, wv, ids_row, ids_col,
    mlp_out, context,
    rs_v, e_v, d_v, t_v, q_v, k_v, v_v,
    part, c_buf, x_buf, z_buf, feats, acc, y_send, y_buf,
    full, pw, r_col, kvp, kvr, kvs, kvt, kv, qacc,
    load_sem, c_sem, x_sem, z_sem, gz_sem, gx_sem, gc_sem, y_sem, f_sem, p_sem, kr_sem, kt_sem, kg_sem,
):
    nx = n // (NC * NZ)
    rows = resid.shape[1]
    share = resid.shape[2]
    fc = enc_w.shape[2] // T
    R = rows // n_src
    H, X, Z = rows // NC, rows // (NC * nx), rows // n
    w = lax.axis_index("width")
    s = lax.axis_index("src")
    c = lax.rem(w, NC)
    x = lax.rem(w // NC, nx)
    z = w // (NC * nx)
    members = 4
    g, m = w // members, lax.rem(w, members)
    n_kv = n // members
    RQ = R // members

    def wid(zz, xx, cc):
        return (zz * nx + xx) * NC + cc

    def plus(v, k, size):
        return lax.rem(v + k, size)

    def minus(v, k, size):
        return lax.rem(v + size - k, size)

    def ds(start, size):
        return pl.ds(pl.multiple_of(start, size), size)

    loads = []

    def load(i, src, dst):
        cp = pltpu.make_async_copy(src, dst, load_sem.at[i])
        cp.start()
        loads.append(cp)
        return cp

    ld_resid = load(0, resid.at[0], rs_v)
    ld_e = [load(1 + t, enc_w.at[0, :, pl.ds(t * fc, fc)], e_v.at[t]) for t in range(T)]
    ld_d = load(T + 1, dec_w.at[0], d_v)
    ld_t = load(T + 2, target.at[ds(s * R, R)], t_v)
    ld_k = load(T + 3, wk, k_v)
    ld_v = load(T + 4, wv, v_v)
    ld_q = load(T + 5, wq, q_v)

    barrier = pltpu.get_barrier_semaphore()
    for k in range(1, n):
        pl.semaphore_signal(barrier, inc=1, device_id={"src": s, "width": plus(w, k, n)})
    for ks in range(1, n_src):
        for mm in range(members):
            pl.semaphore_signal(
                barrier, inc=1,
                device_id={"src": plus(s, ks, n_src), "width": g * members + mm},
            )

    sends = []

    def rdma(src, dst, sems, i, dev):
        return pltpu.make_async_remote_copy(
            src_ref=src, dst_ref=dst, send_sem=sems.at[(0,) + i], recv_sem=sems.at[(1,) + i],
            device_id=dev, device_id_type=pl.DeviceIdType.MESH,
        )

    def send(src, dst, sems, i, ww=None, ss=None):
        cp = rdma(src, dst, sems, i, {"src": s if ss is None else ss, "width": w if ww is None else ww})
        cp.start()
        sends.append(cp)

    def arrive(dst, sems, i):
        rdma(dst, dst, sems, i, {"src": s, "width": plus(w, 1, n)}).wait_recv()

    sibling = wid(z, x, 1 - c)
    c0 = c * H
    x0 = c0 + x * X
    z0 = x0 + z * Z

    def encode(t):
        ld_e[t].wait()
        step = 512 if fc % 512 == 0 else fc

        @pl.loop(0, fc // step)
        def _(j):
            cols = ds(j * step, step)
            part[t, :, cols] = dot(rs_v[...], e_v[t, :, cols]).astype(BF)

    def rs_c(t):
        send(part.at[t, ds((1 - c) * H, H)], c_buf.at[t], c_sem, (t,), sibling)

    def rs_x(t):
        arrive(c_buf.at[t], c_sem, (t,))

        def add(xx):
            @pl.loop(0, X // Z)
            def _(j):
                a = ds(c0 + xx * X + j * Z, Z)
                b = ds(xx * X + j * Z, Z)
                part[t, a] = (part[t, a].astype(F32) + c_buf[t, b].astype(F32)).astype(BF)

        for k in range(1, nx):
            xx = plus(x, k, nx)
            add(xx)
            send(part.at[t, ds(c0 + xx * X, X)], x_buf.at[t, k - 1], x_sem, (t, k - 1), wid(z, xx, c))
        add(x)

    def rs_z(t):
        for k in range(1, nx):
            arrive(x_buf.at[t, k - 1], x_sem, (t, k - 1))

        def add(zz):
            a = ds(x0 + zz * Z, Z)
            b = ds(zz * Z, Z)
            total = part[t, a].astype(F32)
            for k in range(1, nx):
                total += x_buf[t, k - 1, b].astype(F32)
            part[t, a] = total.astype(BF)

        for k in (2, 1, 3):
            zz = plus(z, k, NZ)
            add(zz)
            send(part.at[t, ds(x0 + zz * Z, Z)], z_buf.at[t, k - 1], z_sem, (t, k - 1), wid(zz, x, c))
        add(z)

    def ag_z(t):
        for k in range(1, NZ):
            arrive(z_buf.at[t, k - 1], z_sem, (t, k - 1))
        own = ds(z0, Z)
        total = part[t, own].astype(F32) + enc_b[:, pl.ds(t * fc, fc)]
        for k in range(1, NZ):
            total += z_buf[t, k - 1].astype(F32)
        feats[t, own] = jnp.maximum(total, 0.0).astype(BF)
        for k in (2, 1, 3):
            send(feats.at[t, own], feats.at[t, own], gz_sem, (t, k - 1), wid(plus(z, k, NZ), x, c))

    def ag_x(t):
        for k in range(1, NZ):
            arrive(feats.at[t, ds(x0 + minus(z, k, NZ) * Z, Z)], gz_sem, (t, k - 1))
        own = ds(x0, X)
        for k in range(1, nx):
            send(feats.at[t, own], feats.at[t, own], gx_sem, (t, k - 1), wid(z, plus(x, k, nx), c))

    def ag_c(t):
        for k in range(1, nx):
            arrive(feats.at[t, ds(c0 + minus(x, k, nx) * X, X)], gx_sem, (t, k - 1))
        own = ds(c0, H)
        send(feats.at[t, own], feats.at[t, own], gc_sem, (t,), sibling)

    def decode_rows(t, start):
        r = ds(start, R)
        p = dot(feats[t, r], d_v[pl.ds(t * fc, fc), :])
        if t == 0:
            acc[r, :] = p
        else:
            acc[r, :] += p

    def decode(t):
        arrive(feats.at[t, ds((1 - c) * H, H)], gc_sem, (t,))
        if t == 0:
            ld_d.wait()
        for k in range(1, n_src):
            ss = plus(s, k, n_src)
            decode_rows(t, ss * R)
            if t == T - 1:
                y_send[k - 1] = acc[ds(ss * R, R), :].astype(BF)
                send(y_send.at[k - 1], y_buf.at[k - 1], y_sem, (k - 1,), None, ss)
        decode_rows(t, s * R)

    ld_resid.wait()
    encode(0)
    pl.semaphore_wait(barrier, n - 1 + (n_src - 1) * members)
    rs_c(0)
    for t in range(1, T):
        encode(t)
        rs_c(t)
        rs_x(t - 1)
    rs_x(T - 1)
    stages = (rs_z, ag_z, ag_x, ag_c, decode)
    for tick in range(T + len(stages) - 1):
        for i in range(len(stages)):
            if 0 <= tick - i < T:
                stages[i](tick - i)

    for k in range(1, n_src):
        arrive(y_buf.at[k - 1], y_sem, (k - 1,))
    mlp = acc[ds(s * R, R), :]
    for k in range(1, n_src):
        mlp += y_buf[k - 1].astype(F32)
    mlp_out[...] = mlp.astype(BF)
    ld_t.wait()
    stream = t_v[...].astype(F32) + mlp

    def slot(cc, xx, zz):
        return (cc * nx + xx) * NZ + zz

    me = slot(c, x, z)
    full[me] = (stream * gain[...]).astype(BF)

    def forward(cc_done, kx, kz, at):
        if kx == 0:
            for k in range(1, nx):
                send(full.at[at], full.at[at], f_sem, (0, k, kz), wid(z, plus(x, k, nx), c))
        send(full.at[at], full.at[at], f_sem, (1, kx, kz), sibling)

    for k in (2, 1, 3):
        send(full.at[me], full.at[me], f_sem, (0, 0, k), wid(plus(z, k, NZ), x, c))
    forward(0, 0, 0, me)

    sq = lax.dot_general(
        jnp.ones((8, share), F32), stream * stream, (((1,), (1,)), ((), ())),
        precision=lax.Precision.HIGHEST, preferred_element_type=F32,
    )
    pw[0] = sq
    for k in range(1, n):
        send(pw.at[0], pw.at[k], p_sem, (k - 1,), plus(w, k, n))

    ld_k.wait()
    ld_v.wait()
    kp = dot(full[me], k_v[...]).astype(BF)
    vp = dot(full[me], v_v[...]).astype(BF)
    for mm in range(members):
        for h in range(n_kv):
            kvp[mm, h, :, 0:HD] = kp[mm * RQ:(mm + 1) * RQ, h * HD:(h + 1) * HD]
            kvp[mm, h, :, HD:2 * HD] = vp[mm * RQ:(mm + 1) * RQ, h * HD:(h + 1) * HD]
    for k in (2, 1, 3):
        mm = plus(m, k, members)
        send(kvp.at[mm], kvr.at[k - 1], kr_sem, (k - 1,), g * members + mm)

    def add_query(at, origin):
        qacc[...] += dot(full[at], q_v[ds(origin * share, share), :])

    ld_q.wait()
    qacc[...] = dot(full[me], q_v[ds(w * share, share), :])
    for kz in (1, 2, 3):
        zz = minus(z, kz, NZ)
        at = slot(c, x, zz)
        arrive(full.at[at], f_sem, (0, 0, kz))
        forward(0, 0, kz, at)
        add_query(at, wid(zz, x, c))

    for k in range(1, members):
        arrive(kvr.at[k - 1], kr_sem, (k - 1,))
    group = kvp[m].astype(F32)
    for k in range(1, members):
        group += kvr[k - 1].astype(F32)
    kvs[...] = group.astype(BF)
    for k in range(1, n_kv):
        gg = plus(g, k, n_kv)
        send(kvs.at[gg], kvt.at[k - 1], kt_sem, (k - 1,), gg * members + m)

    for kx in range(1, nx):
        xx = minus(x, kx, nx)
        for kz in range(NZ):
            zz = minus(z, kz, NZ)
            at = slot(c, xx, zz)
            arrive(full.at[at], f_sem, (0, kx, kz))
            forward(0, kx, kz, at)
            add_query(at, wid(zz, xx, c))
    total = pw[0]
    for k in range(1, n):
        arrive(pw.at[k], p_sem, (k - 1,))
    for k in range(1, n):
        total += pw[k]
    r_col[...] = jnp.transpose(lax.rsqrt(total / (share * n) + 1e-05))
    for k in range(1, n_kv):
        arrive(kvt.at[k - 1], kt_sem, (k - 1,))
    mine = kvs[g].astype(F32)
    for k in range(1, n_kv):
        mine += kvt[k - 1].astype(F32)
    out_rows = ds(s * R + m * RQ, RQ)
    kv[out_rows, :] = (mine * r_col[ds(m * RQ, RQ), 0:1]).astype(BF)
    for ks in range(n_src):
        for km in range(members):
            if ks or km:
                send(
                    kv.at[out_rows], kv.at[out_rows], kg_sem, (ks, km),
                    g * members + plus(m, km, members), plus(s, ks, n_src),
                )

    for kx in range(nx):
        xx = minus(x, kx, nx)
        for kz in range(NZ):
            zz = minus(z, kz, NZ)
            at = slot(1 - c, xx, zz)
            arrive(full.at[at], f_sem, (1, kx, kz))
            add_query(at, wid(zz, xx, 1 - c))

    for ks in range(n_src):
        for km in range(members):
            if ks or km:
                at = minus(s, ks, n_src) * R + minus(m, km, members) * RQ
                arrive(kv.at[ds(at, RQ)], kg_sem, (ks, km))

    query = (qacc[...] * r_col[:, 0:1]).astype(BF)
    qi = s * R + lax.broadcasted_iota(jnp.int32, (R, rows), 0)
    ki = lax.broadcasted_iota(jnp.int32, (R, rows), 1)
    allowed = (ids_col[...] == ids_row[...]) & (ki <= qi)
    for h in range(query.shape[1] // HD):
        scores = lax.dot_general(
            query[:, h * HD:(h + 1) * HD], kv[:, 0:HD], (((1,), (1,)), ((), ())),
            preferred_element_type=F32,
        ) * (1.0 / math.sqrt(HD))
        scores = jnp.where(allowed, scores, -1e30)
        peak = jnp.max(scores, axis=-1, keepdims=True)
        weights = jnp.exp(scores - peak)
        probs = (weights / jnp.sum(weights, axis=-1, keepdims=True)).astype(BF)
        context[:, h * HD:(h + 1) * HD] = dot(probs, kv[:, HD:2 * HD]).astype(BF)

    for cp in sends:
        cp.wait_send()


def on_device(resid, enc_w, enc_b, dec_w, target, norm_gain, wq, wk, wv, prompt_ids):
    n = lax.axis_size("width")
    n_src = lax.axis_size("src")
    rows, share = resid.shape[1:]
    fc = enc_w.shape[2] // T
    R = rows // n_src
    nx = n // (NC * NZ)
    H, X, Z = rows // NC, rows // (NC * nx), rows // n
    members = 4
    n_kv = n // members
    RQ = R // members
    ids_col = lax.dynamic_slice_in_dim(prompt_ids, lax.axis_index("src") * R, R, 0)[:, None]
    any_ = pl.BlockSpec(memory_space=pl.ANY)
    vm = pl.BlockSpec(memory_space=pltpu.VMEM)
    dma = pltpu.SemaphoreType.DMA
    nx1 = max(nx - 1, 1)
    ns1 = max(n_src - 1, 1)
    return pl.pallas_call(
        functools.partial(kernel, n, n_src),
        out_shape=(
            jax.ShapeDtypeStruct((R, share), BF),
            jax.ShapeDtypeStruct((R, wq.shape[1]), BF),
        ),
        in_specs=[any_, any_, vm, any_, any_, vm, any_, any_, any_, vm, vm],
        out_specs=(vm, vm),
        scratch_shapes=[
            pltpu.VMEM((rows, share), BF),
            pltpu.VMEM((T, share, fc), BF),
            pltpu.VMEM((T * fc, share), BF),
            pltpu.VMEM((R, share), BF),
            pltpu.VMEM(wq.shape, BF),
            pltpu.VMEM(wk.shape, BF),
            pltpu.VMEM(wv.shape, BF),
            pltpu.VMEM((T, rows, fc), BF),
            pltpu.VMEM((T, H, fc), BF),
            pltpu.VMEM((T, nx1, X, fc), BF),
            pltpu.VMEM((T, NZ - 1, Z, fc), BF),
            pltpu.VMEM((T, rows, fc), BF),
            pltpu.VMEM((rows, share), F32),
            pltpu.VMEM((ns1, R, share), BF),
            pltpu.VMEM((ns1, R, share), BF),
            pltpu.VMEM((n, R, share), BF),
            pltpu.VMEM((n, 8, R), F32),
            pltpu.VMEM((R, 8), F32),
            pltpu.VMEM((members, n_kv, RQ, 2 * HD), BF),
            pltpu.VMEM((members - 1, n_kv, RQ, 2 * HD), BF),
            pltpu.VMEM((n_kv, RQ, 2 * HD), BF),
            pltpu.VMEM((n_kv - 1, RQ, 2 * HD), BF),
            pltpu.VMEM((rows, 2 * HD), BF),
            pltpu.VMEM((R, wq.shape[1]), F32),
            dma((T + 6,)),
            dma((2, T)),
            dma((2, T, nx1)),
            dma((2, T, NZ - 1)),
            dma((2, T, NZ - 1)),
            dma((2, T, nx1)),
            dma((2, T)),
            dma((2, ns1)),
            dma((2, 2, nx, NZ)),
            dma((2, n - 1)),
            dma((2, members - 1)),
            dma((2, n_kv - 1)),
            dma((2, n_src, members)),
        ],
        compiler_params=pltpu.CompilerParams(
            collective_id=0, has_side_effects=True, vmem_limit_bytes=60 * 1024 * 1024
        ),
    )(resid, enc_w, enc_b, dec_w, target, norm_gain[None, :], wq, wk, wv, prompt_ids[None, :], ids_col)


def solution(mesh):
    in_specs = (
        P("src", None, "width"),
        P("src", "width", None),
        P("src", None),
        P("src", None, "width"),
        P(None, "width"),
        P("width"),
        P(None, "width"),
        P("width", None),
        P("width", None),
        P(),
    )
    out_specs = (P("src", "width"), P("src", "width"))
    return jax.shard_map(
        on_device, mesh=mesh, in_specs=in_specs, out_specs=out_specs, check_vma=False
    )
```

```python
import functools
import math

import jax
import jax.numpy as jnp
from jax import lax
from jax.experimental import pallas as pl
from jax.experimental.pallas import tpu as pltpu
from jax.sharding import PartitionSpec as P

HD = 128
GROUP = 8
NC = 2
NZ = 4
T = 6
BF = jnp.bfloat16
F32 = jnp.float32


def dot(a, b):
    return jnp.dot(a, b, preferred_element_type=F32)


def kernel(
    n, n_src,
    resid, enc_w, enc_b, dec_w, target, gain, wq, wk, wv, ids_row, ids_col,
    mlp_out, context,
    rs_v, e_v, d_v, t_v, q_v, k_v, v_v,
    part, c_buf, x_buf, z_buf, feats, acc, y_send, y_buf,
    full, pw, r_col, kvp, kvr, kvs, kvt, kv, qacc,
    load_sem, c_sem, x_sem, z_sem, gz_sem, gx_sem, gc_sem, y_sem, f_sem, p_sem, kr_sem, kt_sem, kg_sem,
):
    nx = n // (NC * NZ)
    rows = resid.shape[1]
    share = resid.shape[2]
    fc = enc_w.shape[2] // T
    R = rows // n_src
    H, X, Z = rows // NC, rows // (NC * nx), rows // n
    w = lax.axis_index("width")
    s = lax.axis_index("src")
    c = lax.rem(w, NC)
    x = lax.rem(w // NC, nx)
    z = w // (NC * nx)
    members = 4
    g, m = w // members, lax.rem(w, members)
    n_kv = n // members
    RQ = R // members

    def wid(zz, xx, cc):
        return (zz * nx + xx) * NC + cc

    def plus(v, k, size):
        return lax.rem(v + k, size)

    def minus(v, k, size):
        return lax.rem(v + size - k, size)

    def ds(start, size):
        return pl.ds(pl.multiple_of(start, size), size)

    loads = []

    def load(i, src, dst):
        cp = pltpu.make_async_copy(src, dst, load_sem.at[i])
        cp.start()
        loads.append(cp)
        return cp

    ld_resid = load(0, resid.at[0], rs_v)
    ld_e = [load(1 + t, enc_w.at[0, :, pl.ds(t * fc, fc)], e_v.at[t]) for t in range(T)]
    ld_d = load(T + 1, dec_w.at[0], d_v)
    ld_t = load(T + 2, target.at[ds(s * R, R)], t_v)
    ld_k = load(T + 3, wk, k_v)
    ld_v = load(T + 4, wv, v_v)
    ld_q = load(T + 5, wq, q_v)

    barrier = pltpu.get_barrier_semaphore()
    for k in range(1, n):
        pl.semaphore_signal(barrier, inc=1, device_id={"src": s, "width": plus(w, k, n)})
    for ks in range(1, n_src):
        for mm in range(members):
            pl.semaphore_signal(
                barrier, inc=1,
                device_id={"src": plus(s, ks, n_src), "width": g * members + mm},
            )

    sends = []

    def rdma(src, dst, sems, i, dev):
        return pltpu.make_async_remote_copy(
            src_ref=src, dst_ref=dst, send_sem=sems.at[(0,) + i], recv_sem=sems.at[(1,) + i],
            device_id=dev, device_id_type=pl.DeviceIdType.MESH,
        )

    def send(src, dst, sems, i, ww=None, ss=None):
        cp = rdma(src, dst, sems, i, {"src": s if ss is None else ss, "width": w if ww is None else ww})
        cp.start()
        sends.append(cp)

    def arrive(dst, sems, i):
        rdma(dst, dst, sems, i, {"src": s, "width": plus(w, 1, n)}).wait_recv()

    sibling = wid(z, x, 1 - c)
    c0 = c * H
    x0 = c0 + x * X
    z0 = x0 + z * Z

    def encode(t):
        ld_e[t].wait()
        step = 512 if fc % 512 == 0 else fc

        @pl.loop(0, fc // step)
        def _(j):
            cols = ds(j * step, step)
            part[t, :, cols] = dot(rs_v[...], e_v[t, :, cols]).astype(BF)

    def rs_c(t):
        send(part.at[t, ds((1 - c) * H, H)], c_buf.at[t], c_sem, (t,), sibling)

    def rs_x(t):
        arrive(c_buf.at[t], c_sem, (t,))

        def add(xx):
            @pl.loop(0, X // Z)
            def _(j):
                a = ds(c0 + xx * X + j * Z, Z)
                b = ds(xx * X + j * Z, Z)
                part[t, a] = (part[t, a].astype(F32) + c_buf[t, b].astype(F32)).astype(BF)

        for k in range(1, nx):
            xx = plus(x, k, nx)
            add(xx)
            send(part.at[t, ds(c0 + xx * X, X)], x_buf.at[t, k - 1], x_sem, (t, k - 1), wid(z, xx, c))
        add(x)

    def rs_z(t):
        for k in range(1, nx):
            arrive(x_buf.at[t, k - 1], x_sem, (t, k - 1))

        def add(zz):
            a = ds(x0 + zz * Z, Z)
            b = ds(zz * Z, Z)
            total = part[t, a].astype(F32)
            for k in range(1, nx):
                total += x_buf[t, k - 1, b].astype(F32)
            part[t, a] = total.astype(BF)

        for k in (2, 1, 3):
            zz = plus(z, k, NZ)
            add(zz)
            send(part.at[t, ds(x0 + zz * Z, Z)], z_buf.at[t, k - 1], z_sem, (t, k - 1), wid(zz, x, c))
        add(z)

    def ag_z(t):
        for k in range(1, NZ):
            arrive(z_buf.at[t, k - 1], z_sem, (t, k - 1))
        own = ds(z0, Z)
        total = part[t, own].astype(F32) + enc_b[:, pl.ds(t * fc, fc)]
        for k in range(1, NZ):
            total += z_buf[t, k - 1].astype(F32)
        feats[t, own] = jnp.maximum(total, 0.0).astype(BF)
        for k in (2, 1, 3):
            send(feats.at[t, own], feats.at[t, own], gz_sem, (t, k - 1), wid(plus(z, k, NZ), x, c))

    def ag_x(t):
        for kz in range(NZ):
            own = ds(x0 + minus(z, kz, NZ) * Z, Z)
            if kz:
                arrive(feats.at[t, own], gz_sem, (t, kz - 1))
            for k in range(1, nx):
                send(feats.at[t, own], feats.at[t, own], gx_sem, (t, k - 1, kz), wid(z, plus(x, k, nx), c))

    def ag_c(t):
        for k in range(1, nx):
            for kz in range(NZ):
                at = c0 + minus(x, k, nx) * X + minus(z, kz, NZ) * Z
                arrive(feats.at[t, ds(at, Z)], gx_sem, (t, k - 1, kz))
        own = ds(c0, H)
        send(feats.at[t, own], feats.at[t, own], gc_sem, (t,), sibling)

    def decode_rows(t, start):
        r = ds(start, R)
        p = dot(feats[t, r], d_v[pl.ds(t * fc, fc), :])
        if t == 0:
            acc[r, :] = p
        else:
            acc[r, :] += p

    def decode(t):
        arrive(feats.at[t, ds((1 - c) * H, H)], gc_sem, (t,))
        if t == 0:
            ld_d.wait()
        for k in range(1, n_src):
            ss = plus(s, k, n_src)
            decode_rows(t, ss * R)
            if t == T - 1:
                y_send[k - 1] = acc[ds(ss * R, R), :].astype(BF)
                send(y_send.at[k - 1], y_buf.at[k - 1], y_sem, (k - 1,), None, ss)
        decode_rows(t, s * R)

    ld_resid.wait()
    encode(0)
    pl.semaphore_wait(barrier, n - 1 + (n_src - 1) * members)
    rs_c(0)
    for t in range(1, T):
        encode(t)
        rs_c(t)
        rs_x(t - 1)
    rs_x(T - 1)
    stages = (rs_z, ag_z, ag_x, ag_c, decode)
    for tick in range(T + len(stages) - 1):
        for i in range(len(stages)):
            if 0 <= tick - i < T:
                stages[i](tick - i)

    for k in range(1, n_src):
        arrive(y_buf.at[k - 1], y_sem, (k - 1,))
    mlp = acc[ds(s * R, R), :]
    for k in range(1, n_src):
        mlp += y_buf[k - 1].astype(F32)
    mlp_out[...] = mlp.astype(BF)
    ld_t.wait()
    stream = t_v[...].astype(F32) + mlp

    def slot(cc, xx, zz):
        return (cc * nx + xx) * NZ + zz

    me = slot(c, x, z)
    full[me] = (stream * gain[...]).astype(BF)

    def forward(cc_done, kx, kz, at):
        if kx == 0:
            for k in range(1, nx):
                send(full.at[at], full.at[at], f_sem, (0, k, kz), wid(z, plus(x, k, nx), c))
        send(full.at[at], full.at[at], f_sem, (1, kx, kz), sibling)

    for k in (2, 1, 3):
        send(full.at[me], full.at[me], f_sem, (0, 0, k), wid(plus(z, k, NZ), x, c))
    forward(0, 0, 0, me)

    sq = lax.dot_general(
        jnp.ones((8, share), F32), stream * stream, (((1,), (1,)), ((), ())),
        precision=lax.Precision.HIGHEST, preferred_element_type=F32,
    )
    pw[0] = sq
    for k in range(1, n):
        send(pw.at[0], pw.at[k], p_sem, (k - 1,), plus(w, k, n))

    ld_k.wait()
    ld_v.wait()
    kp = dot(full[me], k_v[...]).astype(BF)
    vp = dot(full[me], v_v[...]).astype(BF)
    for mm in range(members):
        for h in range(n_kv):
            kvp[mm, h, :, 0:HD] = kp[mm * RQ:(mm + 1) * RQ, h * HD:(h + 1) * HD]
            kvp[mm, h, :, HD:2 * HD] = vp[mm * RQ:(mm + 1) * RQ, h * HD:(h + 1) * HD]
    for k in (2, 1, 3):
        mm = plus(m, k, members)
        send(kvp.at[mm], kvr.at[k - 1], kr_sem, (k - 1,), g * members + mm)

    def add_query(at, origin):
        qacc[...] += dot(full[at], q_v[ds(origin * share, share), :])

    ld_q.wait()
    qacc[...] = dot(full[me], q_v[ds(w * share, share), :])
    for kz in (1, 2, 3):
        zz = minus(z, kz, NZ)
        at = slot(c, x, zz)
        arrive(full.at[at], f_sem, (0, 0, kz))
        forward(0, 0, kz, at)
        add_query(at, wid(zz, x, c))

    for k in range(1, members):
        arrive(kvr.at[k - 1], kr_sem, (k - 1,))
    group = kvp[m].astype(F32)
    for k in range(1, members):
        group += kvr[k - 1].astype(F32)
    kvs[...] = group.astype(BF)
    for k in range(1, n_kv):
        gg = plus(g, k, n_kv)
        send(kvs.at[gg], kvt.at[k - 1], kt_sem, (k - 1,), gg * members + m)

    for kx in range(1, nx):
        xx = minus(x, kx, nx)
        for kz in range(NZ):
            zz = minus(z, kz, NZ)
            at = slot(c, xx, zz)
            arrive(full.at[at], f_sem, (0, kx, kz))
            forward(0, kx, kz, at)
            add_query(at, wid(zz, xx, c))
    total = pw[0]
    for k in range(1, n):
        arrive(pw.at[k], p_sem, (k - 1,))
    for k in range(1, n):
        total += pw[k]
    r_col[...] = jnp.transpose(lax.rsqrt(total / (share * n) + 1e-05))
    for k in range(1, n_kv):
        arrive(kvt.at[k - 1], kt_sem, (k - 1,))
    mine = kvs[g].astype(F32)
    for k in range(1, n_kv):
        mine += kvt[k - 1].astype(F32)
    out_rows = ds(s * R + m * RQ, RQ)
    kv[out_rows, :] = (mine * r_col[ds(m * RQ, RQ), 0:1]).astype(BF)
    for ks in range(n_src):
        for km in range(members):
            if ks or km:
                send(
                    kv.at[out_rows], kv.at[out_rows], kg_sem, (ks, km),
                    g * members + plus(m, km, members), plus(s, ks, n_src),
                )

    for kx in range(nx):
        xx = minus(x, kx, nx)
        for kz in range(NZ):
            zz = minus(z, kz, NZ)
            at = slot(1 - c, xx, zz)
            arrive(full.at[at], f_sem, (1, kx, kz))
            add_query(at, wid(zz, xx, 1 - c))

    for ks in range(n_src):
        for km in range(members):
            if ks or km:
                at = minus(s, ks, n_src) * R + minus(m, km, members) * RQ
                arrive(kv.at[ds(at, RQ)], kg_sem, (ks, km))

    query = (qacc[...] * r_col[:, 0:1]).astype(BF)
    qi = s * R + lax.broadcasted_iota(jnp.int32, (R, rows), 0)
    ki = lax.broadcasted_iota(jnp.int32, (R, rows), 1)
    allowed = (ids_col[...] == ids_row[...]) & (ki <= qi)
    for h in range(query.shape[1] // HD):
        scores = lax.dot_general(
            query[:, h * HD:(h + 1) * HD], kv[:, 0:HD], (((1,), (1,)), ((), ())),
            preferred_element_type=F32,
        ) * (1.0 / math.sqrt(HD))
        scores = jnp.where(allowed, scores, -1e30)
        peak = jnp.max(scores, axis=-1, keepdims=True)
        weights = jnp.exp(scores - peak)
        probs = (weights / jnp.sum(weights, axis=-1, keepdims=True)).astype(BF)
        context[:, h * HD:(h + 1) * HD] = dot(probs, kv[:, HD:2 * HD]).astype(BF)

    for cp in sends:
        cp.wait_send()


def on_device(resid, enc_w, enc_b, dec_w, target, norm_gain, wq, wk, wv, prompt_ids):
    n = lax.axis_size("width")
    n_src = lax.axis_size("src")
    rows, share = resid.shape[1:]
    fc = enc_w.shape[2] // T
    R = rows // n_src
    nx = n // (NC * NZ)
    H, X, Z = rows // NC, rows // (NC * nx), rows // n
    members = 4
    n_kv = n // members
    RQ = R // members
    ids_col = lax.dynamic_slice_in_dim(prompt_ids, lax.axis_index("src") * R, R, 0)[:, None]
    any_ = pl.BlockSpec(memory_space=pl.ANY)
    vm = pl.BlockSpec(memory_space=pltpu.VMEM)
    dma = pltpu.SemaphoreType.DMA
    nx1 = max(nx - 1, 1)
    ns1 = max(n_src - 1, 1)
    return pl.pallas_call(
        functools.partial(kernel, n, n_src),
        out_shape=(
            jax.ShapeDtypeStruct((R, share), BF),
            jax.ShapeDtypeStruct((R, wq.shape[1]), BF),
        ),
        in_specs=[any_, any_, vm, any_, any_, vm, any_, any_, any_, vm, vm],
        out_specs=(vm, vm),
        scratch_shapes=[
            pltpu.VMEM((rows, share), BF),
            pltpu.VMEM((T, share, fc), BF),
            pltpu.VMEM((T * fc, share), BF),
            pltpu.VMEM((R, share), BF),
            pltpu.VMEM(wq.shape, BF),
            pltpu.VMEM(wk.shape, BF),
            pltpu.VMEM(wv.shape, BF),
            pltpu.VMEM((T, rows, fc), BF),
            pltpu.VMEM((T, H, fc), BF),
            pltpu.VMEM((T, nx1, X, fc), BF),
            pltpu.VMEM((T, NZ - 1, Z, fc), BF),
            pltpu.VMEM((T, rows, fc), BF),
            pltpu.VMEM((rows, share), F32),
            pltpu.VMEM((ns1, R, share), BF),
            pltpu.VMEM((ns1, R, share), BF),
            pltpu.VMEM((n, R, share), BF),
            pltpu.VMEM((n, 8, R), F32),
            pltpu.VMEM((R, 8), F32),
            pltpu.VMEM((members, n_kv, RQ, 2 * HD), BF),
            pltpu.VMEM((members - 1, n_kv, RQ, 2 * HD), BF),
            pltpu.VMEM((n_kv, RQ, 2 * HD), BF),
            pltpu.VMEM((n_kv - 1, RQ, 2 * HD), BF),
            pltpu.VMEM((rows, 2 * HD), BF),
            pltpu.VMEM((R, wq.shape[1]), F32),
            dma((T + 6,)),
            dma((2, T)),
            dma((2, T, nx1)),
            dma((2, T, NZ - 1)),
            dma((2, T, NZ - 1)),
            dma((2, T, nx1, NZ)),
            dma((2, T)),
            dma((2, ns1)),
            dma((2, 2, nx, NZ)),
            dma((2, n - 1)),
            dma((2, members - 1)),
            dma((2, n_kv - 1)),
            dma((2, n_src, members)),
        ],
        compiler_params=pltpu.CompilerParams(
            collective_id=0, has_side_effects=True, vmem_limit_bytes=60 * 1024 * 1024
        ),
    )(resid, enc_w, enc_b, dec_w, target, norm_gain[None, :], wq, wk, wv, prompt_ids[None, :], ids_col)


def solution(mesh):
    in_specs = (
        P("src", None, "width"),
        P("src", "width", None),
        P("src", None),
        P("src", None, "width"),
        P(None, "width"),
        P("width"),
        P(None, "width"),
        P("width", None),
        P("width", None),
        P(),
    )
    out_specs = (P("src", "width"), P("src", "width"))
    return jax.shard_map(
        on_device, mesh=mesh, in_specs=in_specs, out_specs=out_specs, check_vma=False
    )
```
